128 devices in a mesh: col: 8 (over x_lo, z), row: 16 (over y, x_hi, core).
Axes of the slice: x: 4 (x_hi: 2, x_lo: 2; x = x_hi * 2 + x_lo), y: 4, z: 4, core: 2. Of those that a mesh axis runs over, the one named last changes fastest.
Arguments:
- matrix: float32 [16384, 16384], P('row', 'col'), may hold values from -6 to 6
- pattern: int32 [64, 4], P('row'), may hold values 0 or 1
- active: int32 [16, 8, 24, 2], P('row', 'col'), may hold values from 0 to 7, as said below
- pivots: int32 [4], replicated, may hold values from 0 to 63, as said below
- lower_inv: float32 [4, 256, 256], replicated, may hold values from -0.3 to 0.3, as said below
- upper_inv: float32 [4, 256, 256], replicated, may hold values from -0.3 to 0.3, as said below
Outputs:
- factored: float32 [16384, 16384], P('row', 'col')
The draws below stay inside these ranges and needn't reach their ends.
Inputs may be any that keep to these rules, and one draw needn't show every extreme that they name: For each device (a, b), active[a, b] holds 24 distinct pairs (l, c) with l below 4 and c below 8. `pivots`: 4 distinct block rows of the window, among them always the first and the last block row. `lower_inv`: each block is lower triangular with a positive diagonal. `upper_inv`: each block is upper triangular with a positive diagonal.
All inputs are finite; a program needn't handle non-finite values. No bound on the sum of `pattern` on one device may be relied on, other than what follows from the above.
Results may differ from the reference program's by a relative error of at most 0.0001.
Values sent between devices are 32-bit elements; how exact they have to be, the bound alone decides.
No kernel may reach another device: no remote copies, remote signals or barrier semaphores. Data moves between devices by JAX's collectives and lax.ppermute only.
A program may use at most 128 MiB of HBM per device.

```python
import jax
import jax.numpy as jnp
from jax import lax

BLOCK_SIZE = 256
PANELS = 4
RL = 4
CL = 8
ACT = 24
PR = 16
PC = 8
NR = 64
NC = 64


def draw_active(key, part):
    device_keys = jax.random.split(jax.random.fold_in(key, 3), PR * PC)

    def one_device(sub_key):
        chosen = jax.random.permutation(sub_key, RL * CL)[:ACT]
        return jnp.stack([chosen // CL, chosen % CL], axis=1).astype(jnp.int32)
    return jax.vmap(one_device)(device_keys).reshape(PR, PC, ACT, 2)


def draw_pivots(key, part):
    middle = jax.random.permutation(jax.random.fold_in(key, 5), NR - 2)[:PANELS - 2].astype(jnp.int32) + 1
    ends = jnp.array([0, NR - 1], dtype=jnp.int32)
    chosen = jnp.concatenate([ends, middle])
    order = jax.random.permutation(jax.random.fold_in(key, 6), PANELS)
    return chosen[order].astype(jnp.int32)


def inverse_blocks(key, lower_side):
    noise_key = jax.random.fold_in(key, 11)
    gain_key = jax.random.fold_in(key, 12)
    noise = jax.random.normal(noise_key, (PANELS, BLOCK_SIZE, BLOCK_SIZE), jnp.float32)
    noise = jnp.clip(noise, -4.0, 4.0) * (0.6 / BLOCK_SIZE ** 0.5)
    if lower_side:
        noise = jnp.tril(noise, -1)
    else:
        noise = jnp.triu(noise, 1)
    gains = jax.random.uniform(gain_key, (PANELS, 1, BLOCK_SIZE), jnp.float32, 0.6, 1.4)
    return 0.2 * (jnp.eye(BLOCK_SIZE, dtype=jnp.float32)[None] * gains + noise)


def draw_lower_inv(key, part):
    return inverse_blocks(jax.random.fold_in(key, 21), True)


def draw_upper_inv(key, part):
    return inverse_blocks(jax.random.fold_in(key, 22), False)


def touch_ends(drawn, key, smallest, largest):
    longest = drawn.shape.index(max(drawn.shape))
    spots = []
    for shift in (0, 1):
        where = [jax.random.randint(jax.random.fold_in(key, axis), (), 0, length) for axis, length in enumerate(drawn.shape)]
        where[longest] = (where[longest] + shift) % drawn.shape[longest]
        spots.append(tuple(where))
    return drawn.at[spots[0]].set(smallest).at[spots[1]].set(largest)


def level_of(rng, dims, pieces, low, largest):
    factor_of = 1.0
    for position, parts in pieces:
        draws = jax.random.uniform(jax.random.fold_in(jax.random.fold_in(rng, 6), position), (parts,), jnp.float32, low / len(pieces), largest / len(pieces))
        factor_of = factor_of * jnp.repeat(jnp.exp(draws), dims[position] // parts).reshape((-1,) + (1,) * (len(dims) - 1 - position))
    return factor_of


def centred(rng, extent, scale, bound, cuts=(), held_as=jnp.bfloat16):
    entries = jax.random.normal(rng, extent, jnp.float32) * scale
    if len(cuts) > 0:
        entries = level_of(rng, extent, cuts, -0.22, 0.18) * entries
    return jnp.clip(entries, min=-bound, max=bound).astype(held_as)


def setup_inputs(seed: int = 0) -> dict:
    arg_keys = jax.random.split(jax.random.key(seed), 7)
    return {
        "matrix": centred(arg_keys[0], (NR * BLOCK_SIZE, NC * BLOCK_SIZE), 1.0, 6.0, ((0, 16), (1, 8)), jnp.float32),
        "pattern": touch_ends((jax.random.randint(arg_keys[1], (NR, PANELS), 0, 4) < 3).astype(jnp.int32), jax.random.fold_in(arg_keys[1], 1), 0, 1),
        "active": draw_active(jax.random.fold_in(arg_keys[6], 71), 0),
        "pivots": draw_pivots(jax.random.fold_in(arg_keys[6], 71), 0),
        "lower_inv": draw_lower_inv(jax.random.fold_in(arg_keys[6], 71), 0),
        "upper_inv": draw_upper_inv(jax.random.fold_in(arg_keys[6], 71), 0),
    }


def reference(matrix, pattern, active, pivots, lower_inv, upper_inv):
    highest = lax.Precision.HIGHEST
    dev_rows = jnp.arange(PR, dtype=jnp.int32)[:, None, None]
    dev_cols = jnp.arange(PC, dtype=jnp.int32)[None, :, None]
    live_rows = (dev_rows * RL + active[:, :, :, 0]).reshape(-1).astype(jnp.int32)
    live_cols = (dev_cols * CL + active[:, :, :, 1]).reshape(-1).astype(jnp.int32)
    remaining_tiles = jnp.zeros((NR, NC), jnp.int32).at[live_rows, live_cols].set(1)
    block_row_count = jnp.arange(NR, dtype=jnp.int32)
    block_cols = jnp.arange(NC, dtype=jnp.int32)
    factored = matrix
    for present_panel in range(PANELS):
        elimination_rows = jnp.any(block_row_count[:, None] == pivots[None, :present_panel + 1], axis=1)
        finished_columns = (block_cols % CL == 0) & (block_cols // CL <= present_panel)
        column = present_panel * CL
        raw_col = factored[:, column * BLOCK_SIZE:(column + 1) * BLOCK_SIZE]
        keep_mask = jnp.repeat((pattern[:, present_panel] != 0).astype(jnp.float32), BLOCK_SIZE)[:, None]
        lower_tile_grid = jnp.dot(raw_col, upper_inv[present_panel], precision=highest, preferred_element_type=jnp.float32) * keep_mask
        pivot_row = pivots[present_panel].astype(jnp.int32)
        raw_row = lax.dynamic_slice_in_dim(factored, pivot_row * BLOCK_SIZE, BLOCK_SIZE, 0)
        upper_tiles = jnp.dot(lower_inv[present_panel], raw_row, precision=highest, preferred_element_type=jnp.float32)
        permitted_entries = (remaining_tiles != 0) & jnp.logical_not(elimination_rows)[:, None] & jnp.logical_not(finished_columns)[None, :]

        def update_row(row_item):
            row_block, low_tile, row_ok = row_item
            product = jnp.dot(low_tile, upper_tiles, precision=highest, preferred_element_type=jnp.float32)
            return row_block - jnp.where(jnp.repeat(row_ok, BLOCK_SIZE)[None, :], product, 0.0)

        updated = lax.map(update_row, (factored.reshape(NR, BLOCK_SIZE, NC * BLOCK_SIZE), lower_tile_grid.reshape(NR, BLOCK_SIZE, BLOCK_SIZE), permitted_entries))
        factored = updated.reshape(NR * BLOCK_SIZE, NC * BLOCK_SIZE)
        column_present = factored[:, column * BLOCK_SIZE:(column + 1) * BLOCK_SIZE]
        fresh_column = jnp.where(jnp.repeat(jnp.logical_not(elimination_rows), BLOCK_SIZE)[:, None], lower_tile_grid, column_present)
        factored = factored.at[:, column * BLOCK_SIZE:(column + 1) * BLOCK_SIZE].set(fresh_column)
        row_now = lax.dynamic_slice_in_dim(factored, pivot_row * BLOCK_SIZE, BLOCK_SIZE, 0)
        new_row = jnp.where(jnp.repeat(jnp.logical_not(finished_columns), BLOCK_SIZE)[None, :], upper_tiles, row_now)
        factored = lax.dynamic_update_slice_in_dim(factored, new_row, pivot_row * BLOCK_SIZE, 0)
    return factored
```

```python
import functools

import jax
import jax.numpy as jnp
from jax import lax
from jax.experimental import pallas as pl
from jax.experimental.pallas import tpu as pltpu
from jax.sharding import Mesh, PartitionSpec as P

PANELS = 4
PAIRS = [(m, p) for m in range(PANELS) for p in range(m + 1, PANELS)]
FLAG_ROWS = 8
MIB = 1024 * 1024


def split(x):
    high = x.astype(jnp.bfloat16)
    return high, (x - high.astype(jnp.float32)).astype(jnp.bfloat16)


def dot3(a, b):
    dot = functools.partial(jnp.dot, preferred_element_type=jnp.float32)
    return dot(a[0], b[0]) + (dot(a[0], b[1]) + dot(a[1], b[0]))


def lower_kernel(scalars, raw, corner, linv, uinv, lh, ll, chosen, ch, cl, *, tile):
    z, core, b = scalars[0], scalars[1], scalars[2]
    half = tile // 2

    def corner_tile(k, m):
        at = lax.rem(z - k + 4, 4)
        return jnp.concatenate([corner[core, at, m, :half], corner[1 - core, at, m, :half]], axis=0)

    def corner_flag(k, m, row):
        return corner[0, lax.rem(z - k + 4, 4), m, half + row : half + row + 1]

    low, up = {}, {}
    uinvs = [split(uinv[k]) for k in range(PANELS)]
    for m in range(PANELS - 1):
        left = split(linv[m])
        for c in range(m + 1, PANELS):
            value = corner_tile(c, m)
            if m:
                total = sum(dot3(low[r, m], up[r, c]) for r in range(m))
                value = value - corner_flag(c, m, 0) * total
            up[m, c] = split(dot3(left, split(value)))
        for p in range(m + 1, PANELS):
            value = corner_tile(m, p)
            if m:
                total = sum(dot3(low[r, p], up[r, m]) for r in range(m))
                value = value - corner_flag(m, p, 0) * total
            low[m, p] = split(dot3(split(value), uinvs[m]) * corner_flag(m, p, 1 + m))
            at = PAIRS.index((m, p))
            ch[at], cl[at] = low[m, p]

    for l in range(4):
        rows = slice(l * tile, (l + 1) * tile)
        done = []
        for k in range(PANELS):
            at = lax.rem(z - k + 4, 4)
            value = raw[at, rows]
            if k:
                flag = raw[at, 4 * tile + l : 4 * tile + l + 1]
                value = value - flag * sum(dot3(done[m], up[m, k]) for m in range(k))
            value = dot3(split(value), uinvs[k]) * scalars[3 + l * PANELS + k].astype(jnp.float32)
            value = jnp.where(scalars[19 + l * PANELS + k] != 0, value, 0.0)
            done.append(split(value))
            columns = slice(k * tile, (k + 1) * tile)
            lh[rows, columns], ll[rows, columns] = done[-1]

            @pl.when(b == k)
            def _():
                chosen[rows] = value


def update_kernel(scalars, raw, linv, lh, ll, chosen, ch, cl, old, new, up, uh, ul, *, tile):
    f = scalars[1]
    done = []
    for k in range(PANELS):
        value = raw[k, :tile]
        if k:
            at = [PAIRS.index((m, k)) for m in range(k)]
            total = sum(dot3((ch[at[m]], cl[at[m]]), done[m]) for m in range(k))
            value = value - raw[k, tile : tile + 1] * total
        value = dot3(split(linv[k]), split(value))
        up[k] = value
        done.append(split(value))
        rows = slice(k * tile, (k + 1) * tile)
        uh[rows] = jnp.where(k < f, done[-1][0], jnp.zeros((), jnp.bfloat16))
        ul[rows] = jnp.where(k < f, done[-1][1], jnp.zeros((), jnp.bfloat16))
    for l in range(4):
        rows = slice(l * tile, (l + 1) * tile)
        e, live = scalars[2 + l], scalars[6 + l] != 0

        @pl.when(e < f)
        def _():
            new[rows] = up[jnp.minimum(e, PANELS - 1)]

        @pl.when(f < e)
        def _():
            new[rows] = chosen[rows]

        @pl.when((e == f) & live)
        def _():
            new[rows] = old[rows] - dot3((lh[rows], ll[rows]), (uh[...], ul[...]))

        @pl.when((e == f) & jnp.logical_not(live))
        def _():
            new[rows] = old[rows]


VMEM = pl.BlockSpec(memory_space=pltpu.VMEM)
SMEM = pl.BlockSpec(memory_space=pltpu.SMEM)


def lower_part(scalars, raw, corner, linv, uinv, tile):
    six = jax.ShapeDtypeStruct((len(PAIRS), tile, tile), jnp.bfloat16)
    big = jax.ShapeDtypeStruct((4 * tile, PANELS * tile), jnp.bfloat16)
    return pl.pallas_call(
        functools.partial(lower_kernel, tile=tile),
        in_specs=[SMEM, VMEM, VMEM, VMEM, VMEM],
        out_specs=[VMEM] * 5,
        out_shape=[big, big, jax.ShapeDtypeStruct((4 * tile, tile), jnp.float32), six, six],
        compiler_params=pltpu.CompilerParams(vmem_limit_bytes=40 * MIB),
        cost_estimate=pl.CostEstimate(flops=3 * 60 * 2 * tile**3, bytes_accessed=20 * MIB, transcendentals=0),
    )(scalars, raw, corner, linv, uinv)


def update_part(scalars, raw, linv, lower, old, tile):
    column = pl.BlockSpec((4 * tile, tile), lambda _, s: (0, s[0]))
    grid = pltpu.PrefetchScalarGridSpec(
        num_scalar_prefetch=1,
        grid=(1,),
        in_specs=[VMEM] * 7 + [column],
        out_specs=column,
        scratch_shapes=[
            pltpu.VMEM((PANELS, tile, tile), jnp.float32),
            pltpu.VMEM((PANELS * tile, tile), jnp.bfloat16),
            pltpu.VMEM((PANELS * tile, tile), jnp.bfloat16),
        ],
    )
    return pl.pallas_call(
        functools.partial(update_kernel, tile=tile),
        grid_spec=grid,
        out_shape=jax.ShapeDtypeStruct(old.shape, old.dtype),
        input_output_aliases={8: 0},
        compiler_params=pltpu.CompilerParams(vmem_limit_bytes=32 * MIB),
        cost_estimate=pl.CostEstimate(flops=3 * 26 * 2 * tile**3, bytes_accessed=8 * MIB, transcendentals=0),
    )(scalars, raw, linv, *lower, old)


def turn(x, axis, distance):
    return lax.ppermute(x, axis, [(i, (i + distance) % 4) for i in range(4)])


def swap(x, axis):
    return lax.ppermute(x, axis, [(0, 1), (1, 0)])


def pick(index, options):
    result = options[-1]
    for i in range(len(options) - 2, -1, -1):
        result = jnp.where(index == i, options[i], result)
    return result


def body(matrix, pattern, active, pivots, lower_inv, upper_inv):
    tile = lower_inv.shape[1]
    xl, z, y, xh, core = (lax.axis_index(n) for n in ("xl", "z", "y", "xh", "core"))
    a, b = (y * 2 + xh) * 2 + core, xl * 4 + z
    last = 16 * 4 - 1
    cells = active[0, 0, :, 0] * 8 + active[0, 0, :, 1]
    live = jnp.any(cells[:, None] == jnp.arange(32, dtype=jnp.int32)[None], axis=0).reshape(4, 8)
    live_f = live.astype(jnp.float32)
    kept = (pattern != 0).astype(jnp.int32)

    middle = (pivots != 0) & (pivots != last)
    rank = jnp.cumsum(middle.astype(jnp.int32))
    q = [jnp.sum(jnp.where(middle & (rank == i + 1), pivots, 0)) for i in range(2)]
    slot_of = jnp.where(pivots == 0, 0, jnp.where(pivots == last, 1, rank + 1))
    q_core, q_xh, q_y = ([(v // 4) % 2 for v in q], [(v // 8) % 2 for v in q], [v // 16 for v in q])
    locals_ = [jnp.where(core == 0, 0, 3)] + [v % 4 for v in q]

    def flag_rows(row, columns):
        alive = jnp.repeat(lax.dynamic_index_in_dim(live_f, row, 0, keepdims=False)[: columns // tile], tile)
        kinds = lax.dynamic_index_in_dim(kept, row, 0, keepdims=False).astype(jnp.float32)
        return jnp.concatenate(
            [alive[None], jnp.broadcast_to(kinds[:, None], (PANELS, columns)), jnp.zeros((3, columns), jnp.float32)]
        )

    def merge(mine, theirs, where_q, where_static):
        return jnp.stack(
            [jnp.where(where_static, mine[0], theirs[0])]
            + [jnp.where(where_q[i], mine[1 + i], theirs[1 + i]) for i in range(2)]
        )

    def order(mine, theirs):
        first = jnp.where(xh == 0, mine[0], theirs[0])
        final = jnp.where(xh == 1, mine[0], theirs[0])
        dyn = [jnp.where(xh == q_xh[i], mine[1 + i], theirs[1 + i]) for i in range(2)]
        slots = [first, final] + dyn
        return jnp.stack([pick(slot_of[k], slots) for k in range(PANELS)])

    static_from = (y - 3 * xh + 4) % 4
    q_from = [(y - q_y[i] + 4) % 4 for i in range(2)]

    piece = tile // 8
    corner_own = []
    for row in locals_:
        data = lax.dynamic_slice(matrix, (row * tile, 0), (tile, tile)).reshape(8, piece, tile)
        flags = jnp.broadcast_to(flag_rows(row, tile)[None], (8, FLAG_ROWS, tile))
        corner_own.append(jnp.concatenate([data, flags], axis=1))
    corner_own = jnp.stack(corner_own, axis=1)
    theirs = swap(lax.dynamic_slice_in_dim(corner_own, (1 - core) * 4, 4, 0), "core")
    mine = lax.dynamic_slice_in_dim(corner_own, core * 4, 4, 0)
    merged = merge(
        jnp.moveaxis(mine, 1, 0), jnp.moveaxis(theirs, 1, 0), [core == c for c in q_core], core == xh
    )
    options = [lax.dynamic_index_in_dim(merged, (y + d) % 4, 1, keepdims=False) for d in range(4)]
    options = [options[0]] + [turn(options[d], "y", d) for d in range(1, 4)]
    corner_piece = jnp.stack(
        [pick(static_from, [o[0] for o in options])]
        + [pick(q_from[i], [o[1 + i] for o in options]) for i in range(2)]
    )
    corner_piece = order(corner_piece, swap(corner_piece, "xh"))
    around = [corner_piece] + [turn(corner_piece, "y", d) for d in range(1, 4)]
    around = [pick((y - s + 4) % 4, around) for s in range(4)]
    half = jnp.concatenate([x[:, :piece] for x in around] + [around[0][:, piece:]], axis=1)
    half = jnp.where(xl == 0, half, lax.ppermute(half, "xl", [(0, 1)]))
    halves = jnp.stack([half] + [turn(half, "z", d) for d in range(1, 4)])
    corner = jnp.stack([halves, swap(halves, "core")])

    side = jnp.concatenate(
        [
            matrix[:, :tile],
            jnp.broadcast_to(jnp.pad(live_f[:, 0], (0, FLAG_ROWS - 4))[:, None], (FLAG_ROWS, tile)),
        ]
    )
    side = jnp.where(xl == 0, side, lax.ppermute(side, "xl", [(0, 1)]))
    sides = jnp.stack([side] + [turn(side, "z", d) for d in range(1, 4)])

    wide = 8 * tile
    rows_own = jnp.stack(
        [
            jnp.concatenate([lax.dynamic_slice(matrix, (row * tile, 0), (tile, wide)), flag_rows(row, wide)])
            for row in locals_
        ]
    )
    theirs = swap(lax.dynamic_slice_in_dim(rows_own, (1 - core) * 4 * tile, 4 * tile, 2), "core")
    mine = lax.dynamic_slice_in_dim(rows_own, core * 4 * tile, 4 * tile, 2)
    merged = merge(mine, theirs, [core == c for c in q_core], core == xh)
    options = [lax.dynamic_slice_in_dim(merged, (y + d) % 4 * tile, tile, 2) for d in range(4)]
    options = [(options[0][0], options[0][1:])] + [
        (
            lax.ppermute(options[d][0], ("y", "xh"), [(0, d * 2), (7, (3 + d) % 4 * 2 + 1)]),
            turn(options[d][1:], "y", d),
        )
        for d in range(1, 4)
    ]
    mine = jnp.stack(
        [pick(static_from, [o[0] for o in options])]
        + [pick(q_from[i], [o[1][i] for o in options]) for i in range(2)]
    )
    item = order(mine, swap(mine, "xh"))
    items = [item] + [turn(item, "y", d) for d in range(1, 4)]
    others = [swap(x, "core") for x in items]

    i = a * 4 + jnp.arange(4, dtype=jnp.int32)
    hit = i[:, None] == pivots[None]
    ends = jnp.min(jnp.where(hit, jnp.arange(PANELS, dtype=jnp.int32)[None], PANELS), axis=1)
    keep = (ends[:, None] > jnp.arange(PANELS, dtype=jnp.int32)[None]).astype(jnp.int32)
    scalars = jnp.concatenate([jnp.stack([z, core, b]).astype(jnp.int32), kept.reshape(-1), keep.reshape(-1)])
    lower = lower_part(scalars, sides, corner, lower_inv, upper_inv, tile)
    out = matrix
    for d in range(4):
        for c, data in ((core, items[d]), (1 - core, others[d])):
            j = c * 4 + (y - d + 4) % 4
            f = jnp.where((j == 0) & (b < PANELS), b, PANELS)
            alive = lax.dynamic_index_in_dim(live.astype(jnp.int32), j, 1, keepdims=False)
            scalars = jnp.concatenate([jnp.stack([j, f]).astype(jnp.int32), ends, alive])
            out = update_part(scalars, data, lower_inv, lower, out, tile)
    return out


def solution(mesh):
    fine = Mesh(mesh.devices.reshape(2, 4, 4, 2, 2), ("xl", "z", "y", "xh", "core"))
    row, col = ("y", "xh", "core"), ("xl", "z")
    in_specs = (P(row, col), P(row, None), P(row, col, None, None), P(), P(), P())
    return jax.shard_map(body, mesh=fine, in_specs=in_specs, out_specs=P(row, col), check_vma=False)
```

```python
import functools

import jax
import jax.numpy as jnp
from jax import lax
from jax.experimental import pallas as pl
from jax.experimental.pallas import tpu as pltpu
from jax.sharding import Mesh, PartitionSpec as P

PANELS = 4
PAIRS = [(m, p) for m in range(PANELS) for p in range(m + 1, PANELS)]
FLAG_ROWS = 8
MIB = 1024 * 1024


def split(x):
    high = x.astype(jnp.bfloat16)
    return high, (x - high.astype(jnp.float32)).astype(jnp.bfloat16)


def dot3(a, b):
    dot = functools.partial(jnp.dot, preferred_element_type=jnp.float32)
    return dot(a[0], b[0]) + (dot(a[0], b[1]) + dot(a[1], b[0]))


def place():
    return tuple(lax.axis_index(n) for n in ("xl", "z", "y", "xh", "core"))


def middle_pivots(pivots, last):
    first = second = jnp.int32(-1)
    for k in range(PANELS):
        p = pivots[k]
        inside = (p != 0) & (p != last)
        second = jnp.where(inside & (first >= 0), p, second)
        first = jnp.where(inside & (first < 0), p, first)
    return first, second


def panel_of(pivots, row):
    result = jnp.int32(PANELS)
    for k in range(PANELS - 1, -1, -1):
        result = jnp.where(pivots[k] == row, k, result)
    return result


def lower_kernel(pivots, pattern, raw0, raw1, raw2, raw3, mine, theirs, linv, uinv, lh, ll, chosen, ch, cl, *, tile):
    xl, z, y, xh, core = place()
    b = xl * 4 + z
    ends = [panel_of(pivots, ((y * 2 + xh) * 2 + core) * 4 + l) for l in range(4)]
    piece = tile // 8

    def corner_tile(k, m):
        def rows(c):
            at = pl.ds((m - (m > k)) * piece, piece)
            dz = lax.rem(z - k + 4, 4)
            near = jnp.concatenate([mine[dz, lax.rem(y - t + 4, 4), at] for t in range(4)], axis=0)
            far = jnp.concatenate([theirs[dz, lax.rem(y - t + 4, 4), at] for t in range(4)], axis=0)
            return jnp.where(core == c, near, far)

        return jnp.concatenate([rows(0), rows(1)], axis=0)

    def corner_flag(k, row):
        at = (PANELS - 1) * piece + row
        return mine[lax.rem(z - k + 4, 4), 0, at : at + 1]

    low, up = {}, {}
    uinvs = [split(uinv[k]) for k in range(PANELS)]
    for m in range(PANELS - 1):
        left = split(linv[m])
        for c in range(m + 1, PANELS):
            value = corner_tile(c, m)
            if m:
                total = sum(dot3(low[r, m], up[r, c]) for r in range(m))
                value = value - corner_flag(c, m) * total
            up[m, c] = split(dot3(left, split(value)))
        for p in range(m + 1, PANELS):
            value = corner_tile(m, p)
            if m:
                total = sum(dot3(low[r, p], up[r, m]) for r in range(m))
                value = value - corner_flag(m, p) * total
            low[m, p] = split(dot3(split(value), uinvs[m]) * corner_flag(m, PANELS + p))
            at = PAIRS.index((m, p))
            ch[at], cl[at] = low[m, p]

    def choose(at, rows):
        return pick(at, [raw[rows] for raw in (raw0, raw1, raw2, raw3)])

    def by_row(values):
        return jnp.concatenate([jnp.broadcast_to(v, (tile, tile)) for v in values], axis=0)

    done = []
    for k in range(PANELS):
        at = lax.rem(z - k + 4, 4)
        value = choose(at, slice(0, 4 * tile))
        if k:
            flag = by_row([choose(at, slice(4 * tile + l, 4 * tile + l + 1)) for l in range(4)])
            value = value - flag * sum(dot3(done[m], up[m, k]) for m in range(k))
        value = dot3(split(value), uinvs[k])
        here = [(pattern[l, k] != 0) & (ends[l] > k) for l in range(4)]
        value = jnp.concatenate(
            [jnp.where(here[l], value[l * tile : (l + 1) * tile], 0.0) for l in range(4)], axis=0
        )
        done.append(split(value))
        columns = slice(k * tile, (k + 1) * tile)
        lh[:, columns], ll[:, columns] = done[-1]

        @pl.when(b == k)
        def _():
            chosen[...] = value


def update_kernel(pivots, alive, raw_a, raw_b, linv, lh, ll, chosen, ch, cl, old, *rest, tile, distance):
    xl, z, y, xh, core = place()
    b, t = xl * 4 + z, lax.rem(y + 4 - distance, 4)
    js = [core * 4 + t, (1 - core) * 4 + t]
    fs = [jnp.where((j == 0) & (b < PANELS), b, PANELS) for j in js]
    ends = [panel_of(pivots, ((y * 2 + xh) * 2 + core) * 4 + l) for l in range(4)]
    new, block, up, uh, ul, sems = rest[-6:]
    loads, stores = [], []
    for n in range(2):
        columns = pl.ds(pl.multiple_of(js[n] * tile, tile), tile)
        loads.append(pltpu.make_async_copy(old.at[:, columns], block.at[n], sems.at[n]))
        stores.append(pltpu.make_async_copy(block.at[n], new.at[:, columns], sems.at[2 + n]))
        loads[n].start()
    done = []
    for k in range(PANELS):
        value = jnp.concatenate([raw_a[k, :tile], raw_b[k, :tile]], axis=1)
        if k:
            at = [PAIRS.index((m, k)) for m in range(k)]
            total = sum(dot3((ch[at[m]], cl[at[m]]), done[m]) for m in range(k))
            flag = jnp.concatenate([raw_a[k, tile : tile + 1], raw_b[k, tile : tile + 1]], axis=1)
            value = value - flag * total
        value = dot3(split(linv[k]), split(value))
        done.append(split(value))
        rows = slice(k * tile, (k + 1) * tile)
        for n in range(2):
            columns = slice(n * tile, (n + 1) * tile)
            used = k < fs[n]
            up[n, k] = value[:, columns]
            uh[n, rows] = jnp.where(used, done[-1][0][:, columns], jnp.zeros((), jnp.bfloat16))
            ul[n, rows] = jnp.where(used, done[-1][1][:, columns], jnp.zeros((), jnp.bfloat16))
    for n in range(2):
        loads[n].wait()
        f = fs[n]
        for l in range(4):
            rows = slice(l * tile, (l + 1) * tile)
            e, live = ends[l], alive[l * 8 + js[n]] != 0

            @pl.when(e < f)
            def _():
                block[n, rows] = up[n, jnp.minimum(e, PANELS - 1)]

            @pl.when(f < e)
            def _():
                block[n, rows] = chosen[rows]

            @pl.when((e == f) & live)
            def _():
                block[n, rows] -= dot3((lh[rows], ll[rows]), (uh[n], ul[n]))

        stores[n].start()
    for n in range(2):
        stores[n].wait()


def pack_kernel(pivots, pattern, active, matrix, mine, theirs, corner_mine, corner_theirs, side, alive, sems, *, tile, last):
    core = place()[-1]
    piece, wide = tile // 8, 4 * tile
    rows = [jnp.where(core == 0, 0, 3)] + [lax.rem(q, 4) for q in middle_pivots(pivots, last)]
    copies = [(matrix.at[:, pl.ds(0, tile)], side.at[pl.ds(0, 4 * tile)])]
    outs = ((core, mine, corner_mine), (1 - core, theirs, corner_theirs))
    for s in range(3):
        row = rows[s] * tile
        for half, rows_out, corner_out in outs:
            columns = pl.ds(pl.multiple_of(half * wide, wide), wide)
            for t in range(4):
                start = pl.multiple_of(row + (half * 4 + t) * piece, piece)
                copies.append((matrix.at[pl.ds(start, piece), pl.ds(0, tile)], corner_out.at[t, s, pl.ds(0, piece)]))
            copies.append((matrix.at[pl.ds(pl.multiple_of(row, tile), tile), columns], rows_out.at[s, pl.ds(0, tile)]))
    copies = [pltpu.make_async_copy(*c, sems.at[n]) for n, c in enumerate(copies)]
    for c in copies:
        c.start()
    for n in range(32):
        alive[n] = 0
    for n in range(active.shape[0]):
        alive[active[n, 0] * 8 + active[n, 1]] = 1
    sub = lax.broadcasted_iota(jnp.int32, (FLAG_ROWS, wide), 0)
    for half, rows_out, corner_out in outs:
        block = lax.broadcasted_iota(jnp.int32, (FLAG_ROWS, wide), 1) // tile + half * 4
        for s in range(3):
            flags = jnp.zeros((FLAG_ROWS, wide), jnp.float32)
            for n in range(active.shape[0]):
                hit = (active[n, 0] == rows[s]) & (active[n, 1] == block) & (sub == 0)
                flags = jnp.where(hit, 1.0, flags)
            for n in range(PANELS):
                kind = jnp.where(pattern[rows[s], n] != 0, 1.0, 0.0)
                flags = jnp.where(sub == 1 + n, kind, flags)
            rows_out[s, tile:] = flags
    sub = lax.broadcasted_iota(jnp.int32, (FLAG_ROWS, tile), 0)
    flags = jnp.zeros((FLAG_ROWS, tile), jnp.float32)
    for n in range(active.shape[0]):
        flags = jnp.where((active[n, 0] == sub) & (active[n, 1] == 0), 1.0, flags)
    side[4 * tile :] = flags
    for s in range(3):
        first = jnp.where(core == 0, mine[s, tile:, :tile], theirs[s, tile:, :tile])
        for t in range(4):
            corner_mine[t, s, piece:] = first
            corner_theirs[t, s, piece:] = first
    for c in copies:
        c.wait()


def copy_one(out, index, options):
    for n, option in enumerate(options):

        @pl.when(index == n)
        def _():
            out[...] = option[...]


def cut_kernel(pivots, mine, theirs, own, *sends, tile, last, axis):
    _, _, y, xh, core = place()
    q = middle_pivots(pivots, last)
    near = [core == xh] + [lax.rem(v // 4, 2) == core for v in q]
    for d in range(4):
        t = lax.rem(y + d, 4)
        for s in range(3):
            if d == 0:
                out = own.at[s]
            elif axis == 0:
                out = sends[d - 1].at[s]
            else:
                out = sends[d + 2].at[:] if s == 0 else sends[d - 1].at[s - 1]
            at = (t, s) if axis == 0 else (s, slice(None), pl.ds(pl.multiple_of(t * tile, tile), tile))
            copy_one(out, jnp.where(near[s], 0, 1), [mine.at[at], theirs.at[at]])


def gather_kernel(pivots, own, *rest, last, axis):
    _, _, y, xh, _ = place()
    q = middle_pivots(pivots, last)
    source = [3 * xh] + [v // 16 for v in q]
    out = rest[-1]
    for s in range(3):
        if axis == 0:
            options = [own.at[s]] + [r.at[s] for r in rest[:3]]
        elif s == 0:
            options = [own.at[s]] + [r.at[:] for r in rest[3:6]]
        else:
            options = [own.at[s]] + [r.at[s - 1] for r in rest[:3]]
        copy_one(out.at[s], lax.rem(y - source[s] + 4, 4), options)


def slots_of(pivots, last):
    _, _, _, xh, _ = place()
    q = middle_pivots(pivots, last)
    result = []
    for k in range(PANELS):
        p = pivots[k]
        which = jnp.where((p == 0) | (p == last), 0, jnp.where(p == q[0], 1, 2))
        result.append(which + jnp.where(lax.rem(p // 8, 2) == xh, 0, 3))
    return result


def order_kernel(pivots, mine, theirs, out, *, last):
    for k, slot in enumerate(slots_of(pivots, last)):
        copy_one(out.at[k], slot, [mine.at[s] for s in range(3)] + [theirs.at[s] for s in range(3)])


def order_corner_kernel(pivots, mine, theirs, out, *, piece, last):
    z = place()[1]
    for k, slot in enumerate(slots_of(pivots, last)):
        for n in range(6):
            source = (mine if n < 3 else theirs).at[n % 3]

            @pl.when((slot == n) & (z != k))
            def _():
                at = pl.multiple_of((k - jnp.where(z < k, 1, 0)) * piece, 8)
                out[pl.ds(at, piece)] = source[:piece]

            @pl.when(slot == n)
            def _():
                at = (PANELS - 1) * piece + k
                out[at : at + 1] = source[piece : piece + 1]
                out[at + PANELS : at + PANELS + 1] = source[pl.ds(piece + 1 + z, 1)]


VMEM = pl.BlockSpec(memory_space=pltpu.VMEM)
SMEM = pl.BlockSpec(memory_space=pltpu.SMEM)
ANY = pl.BlockSpec(memory_space=pl.ANY)
HBM = pl.BlockSpec(memory_space=pltpu.HBM)


def small(kernel, pivots, arrays, shapes, **sizes):
    return pl.pallas_call(
        functools.partial(kernel, **sizes),
        in_specs=[SMEM] + [VMEM] * len(arrays),
        out_specs=[VMEM] * len(shapes),
        out_shape=[jax.ShapeDtypeStruct(s, jnp.float32) for s in shapes],
        compiler_params=pltpu.CompilerParams(vmem_limit_bytes=24 * MIB),
    )(pivots, *arrays)


def pack(pivots, pattern, active, matrix, tile, last):
    def shape(*dims):
        return jax.ShapeDtypeStruct(dims, jnp.float32)

    rows = shape(3, tile + FLAG_ROWS, 4 * tile)
    pieces = shape(4, 3, tile // 8 + FLAG_ROWS, tile)
    alive = jax.ShapeDtypeStruct((32,), jnp.int32)
    return pl.pallas_call(
        functools.partial(pack_kernel, tile=tile, last=last),
        in_specs=[SMEM] * 3 + [HBM],
        out_specs=[VMEM] * 5 + [SMEM],
        out_shape=[rows, rows, pieces, pieces, shape(4 * tile + FLAG_ROWS, tile), alive],
        scratch_shapes=[pltpu.SemaphoreType.DMA((31,))],
        compiler_params=pltpu.CompilerParams(vmem_limit_bytes=40 * MIB),
    )(pivots, pattern, active, matrix)


def lower_part(pivots, pattern, sides, corner, linv, uinv, tile):
    six = jax.ShapeDtypeStruct((len(PAIRS), tile, tile), jnp.bfloat16)
    big = jax.ShapeDtypeStruct((4 * tile, PANELS * tile), jnp.bfloat16)
    return pl.pallas_call(
        functools.partial(lower_kernel, tile=tile),
        in_specs=[SMEM] * 2 + [VMEM] * 8,
        out_specs=[VMEM] * 5,
        out_shape=[big, big, jax.ShapeDtypeStruct((4 * tile, tile), jnp.float32), six, six],
        compiler_params=pltpu.CompilerParams(vmem_limit_bytes=40 * MIB),
        cost_estimate=pl.CostEstimate(flops=3 * 150 * 2 * tile**3, bytes_accessed=20 * MIB, transcendentals=0),
    )(pivots, pattern, *sides, *corner, linv, uinv)


def update_part(pivots, alive, raw_a, raw_b, linv, lower, old, partial, tile, distance):
    given = [] if partial is None else [partial]
    return pl.pallas_call(
        functools.partial(update_kernel, tile=tile, distance=distance),
        in_specs=[SMEM] * 2 + [VMEM] * 8 + [HBM] * (1 + len(given)),
        out_specs=HBM,
        out_shape=jax.ShapeDtypeStruct(old.shape, old.dtype),
        scratch_shapes=[
            pltpu.VMEM((2, 4 * tile, tile), jnp.float32),
            pltpu.VMEM((2, PANELS, tile, tile), jnp.float32),
            pltpu.VMEM((2, PANELS * tile, tile), jnp.bfloat16),
            pltpu.VMEM((2, PANELS * tile, tile), jnp.bfloat16),
            pltpu.SemaphoreType.DMA((4,)),
        ],
        input_output_aliases={11: 0} if given else {},
        compiler_params=pltpu.CompilerParams(vmem_limit_bytes=32 * MIB),
        cost_estimate=pl.CostEstimate(flops=3 * 90 * 2 * tile**3, bytes_accessed=8 * MIB, transcendentals=0),
    )(pivots, alive, raw_a, raw_b, linv, *lower, old, *given)


def turn(x, axis, distance):
    return lax.ppermute(x, axis, [(i, (i + distance) % 4) for i in range(4)])


def swap(x, axis):
    return lax.ppermute(x, axis, [(0, 1), (1, 0)])


def pick(index, options):
    result = options[-1]
    for i in range(len(options) - 2, -1, -1):
        result = jnp.where(index == i, options[i], result)
    return result


def after(x, *others):
    return lax.optimization_barrier((x, others))[0]


def body(matrix, pattern, active, pivots, lower_inv, upper_inv):
    tile = lower_inv.shape[1]
    piece = tile // 8
    xl = lax.axis_index("xl")
    last = 16 * 4 - 1
    packed = pack(pivots, pattern, active[0, 0], matrix, tile, last)
    rows_mine, rows_theirs, corner_mine, corner_theirs, side, alive = packed

    corner_theirs = swap(corner_theirs, "core")
    rows_theirs = swap(rows_theirs, "core")
    side = jnp.where(xl == 0, side, lax.ppermute(side, "xl", [(0, 1)]))
    small_slots = (3, piece + FLAG_ROWS, tile)
    own_c, *sends_c = small(
        cut_kernel, pivots, (corner_mine, corner_theirs), [small_slots] * 4, tile=tile, last=last, axis=0
    )
    recv_c = [turn(x, "y", d + 1) for d, x in enumerate(sends_c)]
    one = (tile + FLAG_ROWS, tile)
    own, *sends = small(
        cut_kernel,
        pivots,
        (after(rows_mine, own_c), rows_theirs),
        [(3, *one)] + [(2, *one)] * 3 + [one] * 3,
        tile=tile,
        last=last,
        axis=2,
    )
    recv = [turn(x, "y", d + 1) for d, x in enumerate(sends[:3])]
    recv += [
        lax.ppermute(x, ("y", "xh"), [(0, d * 2 + 2), (7, d % 4 * 2 + 1)]) for d, x in enumerate(sends[3:])
    ]
    (slots_c,) = small(gather_kernel, pivots, (after(own_c, own), *recv_c), [small_slots], last=last, axis=0)
    slots_c, side = lax.optimization_barrier((slots_c, side))
    near = [turn(side, "z", 1), turn(side, "z", 3)]
    (corner,) = small(
        order_corner_kernel,
        pivots,
        (slots_c, swap(slots_c, "xh")),
        [(3 * piece + FLAG_ROWS, tile)],
        piece=piece,
        last=last,
    )
    corner_y = [corner] + [turn(corner, "y", d) for d in range(1, 4)]
    corner_y = jnp.stack(corner_y)
    corner_y = jnp.where(xl == 0, corner_y, lax.ppermute(corner_y, "xl", [(0, 1)]))
    (slots,) = small(gather_kernel, pivots, (after(own, near, corner_y), *recv), [(3, *one)], last=last, axis=2)
    other_slots = swap(slots, "xh")
    far = turn(side, "z", 2)
    corner_z = jnp.stack([corner_y] + [turn(corner_y, "z", d) for d in range(1, 4)])
    (item,) = small(order_kernel, pivots, (after(slots, far, corner_z), other_slots), [(4, *one)], last=last)
    sides = [side, near[0], far, near[1]]
    items = [item, turn(item, "y", 1), None, turn(item, "y", 3)]
    lower = lower_part(pivots, pattern, sides, (corner_z, swap(corner_z, "core")), lower_inv, upper_inv, tile)
    items[2] = turn(after(item, *lower), "y", 2)
    out = None
    for d in (0, 1, 3, 2):
        mine = after(items[d], out) if d == 2 else items[d]
        other = swap(mine, "core")
        out = update_part(pivots, alive, mine, other, lower_inv, lower, matrix, out, tile, d)
    return out


def solution(mesh):
    fine = Mesh(mesh.devices.reshape(2, 4, 4, 2, 2), ("xl", "z", "y", "xh", "core"))
    row, col = ("y", "xh", "core"), ("xl", "z")
    in_specs = (P(row, col), P(row, None), P(row, col, None, None), P(), P(), P())
    return jax.shard_map(body, mesh=fine, in_specs=in_specs, out_specs=P(row, col), check_vma=False)
```

```python
import functools

import jax
import jax.numpy as jnp
from jax import lax
from jax.experimental import pallas as pl
from jax.experimental.pallas import tpu as pltpu
from jax.sharding import Mesh, PartitionSpec as P

PANELS = 4
PAIRS = [(m, p) for m in range(PANELS) for p in range(m + 1, PANELS)]
FLAG_ROWS = 8
MIB = 1024 * 1024


def split(x):
    high = x.astype(jnp.bfloat16)
    return high, (x - high.astype(jnp.float32)).astype(jnp.bfloat16)


def dot3(a, b):
    dot = functools.partial(jnp.dot, preferred_element_type=jnp.float32)
    return dot(a[0], b[0]) + (dot(a[0], b[1]) + dot(a[1], b[0]))


def place():
    return tuple(lax.axis_index(n) for n in ("xl", "z", "y", "xh", "core"))


def middle_pivots(pivots, last):
    first = second = jnp.int32(-1)
    for k in range(PANELS):
        p = pivots[k]
        inside = (p != 0) & (p != last)
        second = jnp.where(inside & (first >= 0), p, second)
        first = jnp.where(inside & (first < 0), p, first)
    return first, second


def panel_of(pivots, row):
    result = jnp.int32(PANELS)
    for k in range(PANELS - 1, -1, -1):
        result = jnp.where(pivots[k] == row, k, result)
    return result


def lower_kernel(pivots, pattern, *refs, tile):
    given, (lh, ll, chosen, ch, cl), held, sems = refs[:8], refs[8:13], refs[13:21], refs[21]
    copies = [pltpu.make_async_copy(g, h, sems.at[n]) for n, (g, h) in enumerate(zip(given, held))]
    for n in (4, 5, 6, 7, 0, 1, 2, 3):
        copies[n].start()
    raw0, raw1, raw2, raw3, mine, theirs, linv, uinv = held
    xl, z, y, xh, core = place()
    b = xl * 4 + z
    ends = [panel_of(pivots, ((y * 2 + xh) * 2 + core) * 4 + l) for l in range(4)]
    piece = tile // 8

    def corner_tile(k, m):
        def rows(c):
            at = pl.ds((m - (m > k)) * piece, piece)
            dz = lax.rem(z - k + 4, 4)
            near = jnp.concatenate([mine[dz, lax.rem(y - t + 4, 4), at] for t in range(4)], axis=0)
            far = jnp.concatenate([theirs[dz, lax.rem(y - t + 4, 4), at] for t in range(4)], axis=0)
            return jnp.where(core == c, near, far)

        return jnp.concatenate([rows(0), rows(1)], axis=0)

    def corner_flag(k, row):
        at = (PANELS - 1) * piece + row
        return mine[lax.rem(z - k + 4, 4), 0, at : at + 1]

    for n in range(4, 8):
        copies[n].wait()
    uinvs = [split(uinv[k]) for k in range(PANELS)]
    linvs = [split(linv[k]) for k in range(PANELS)]
    pairs = [(m, p) for m in range(PANELS) for p in range(m + 1, PANELS)]
    high = {(m, c): corner_tile(c, m) for m, c in pairs}
    wide = {(m, p): corner_tile(m, p) for m, p in pairs}
    low, up, left, right = {}, {}, {}, {}
    for m in range(PANELS - 1):
        for n in range(m + 1, PANELS):
            u, l = high[m, n], wide[m, n]
            if m:
                u = u - corner_flag(n, m) * sum(dot3(left[r, m], up[r, n]) for r in range(m))
                l = l - corner_flag(m, n) * sum(dot3(low[r, n], right[r, m]) for r in range(m))
            up[m, n] = split(u)
            low[m, n] = split(l * corner_flag(m, PANELS + n))
        for n in range(m + 1, PANELS):
            left[m, n] = split(dot3(linvs[n], low[m, n]))
            right[m, n] = split(dot3(up[m, n], uinvs[n]))
            at = PAIRS.index((m, n))
            ch[at], cl[at] = left[m, n]

    def choose(at, rows):
        return pick(at, [raw[rows] for raw in (raw0, raw1, raw2, raw3)])

    def by_row(values):
        return jnp.concatenate([jnp.broadcast_to(v, (tile, tile)) for v in values], axis=0)

    for n in range(4):
        copies[n].wait()
    done = []
    for k in range(PANELS):
        at = lax.rem(z - k + 4, 4)
        value = choose(at, slice(0, 4 * tile))
        if k:
            flag = by_row([choose(at, slice(4 * tile + l, 4 * tile + l + 1)) for l in range(4)])
            value = value - flag * sum(dot3(done[m], right[m, k]) for m in range(k))
        here = [(pattern[l, k] != 0) & (ends[l] > k) for l in range(4)]
        value = jnp.concatenate(
            [jnp.where(here[l], value[l * tile : (l + 1) * tile], 0.0) for l in range(4)], axis=0
        )
        done.append(split(value))
        columns = slice(k * tile, (k + 1) * tile)
        lh[:, columns], ll[:, columns] = done[-1]

        @pl.when(b == k)
        def _():
            chosen[...] = value


def update_kernel(pivots, alive, *refs, tile, distance, parts):
    raw_a, raw_b = refs[:parts], refs[parts : 2 * parts]
    lh, ll, chosen, ch, cl, old = refs[2 * parts : 2 * parts + 6]
    rest = refs[2 * parts + 6 :]
    each = PANELS // parts
    xl, z, y, xh, core = place()
    b, t = xl * 4 + z, lax.rem(y + 4 - distance, 4)
    js = [core * 4 + t, (1 - core) * 4 + t]
    fs = [jnp.where((j == 0) & (b < PANELS), b, PANELS) for j in js]
    ends = [panel_of(pivots, ((y * 2 + xh) * 2 + core) * 4 + l) for l in range(4)]
    new, block, up, uh, ul, sems = rest[-6:]
    loads, stores = [], []
    for n in range(2):
        columns = pl.ds(pl.multiple_of(js[n] * tile, tile), tile)
        loads.append(pltpu.make_async_copy(old.at[:, columns], block.at[n], sems.at[n]))
        stores.append(pltpu.make_async_copy(block.at[n], new.at[:, columns], sems.at[2 + n]))
        loads[n].start()
    done = []
    for k in range(PANELS):
        pair = [raw[k // each].at[k % each] for raw in (raw_a, raw_b)]
        value = jnp.concatenate([r[:tile] for r in pair], axis=1)
        if k:
            at = [PAIRS.index((m, k)) for m in range(k)]
            total = sum(dot3((ch[at[m]], cl[at[m]]), done[m]) for m in range(k))
            value = value - jnp.concatenate([r[tile : tile + 1] for r in pair], axis=1) * total
        done.append(split(value))
        rows = slice(k * tile, (k + 1) * tile)
        for n in range(2):
            columns = slice(n * tile, (n + 1) * tile)
            used = k < fs[n]
            up[n, k] = value[:, columns]
            uh[n, rows] = jnp.where(used, done[-1][0][:, columns], jnp.zeros((), jnp.bfloat16))
            ul[n, rows] = jnp.where(used, done[-1][1][:, columns], jnp.zeros((), jnp.bfloat16))
    for n in range(2):
        loads[n].wait()
        f = fs[n]
        for l in range(4):
            rows = slice(l * tile, (l + 1) * tile)
            e, live = ends[l], alive[l * 8 + js[n]] != 0

            @pl.when(e < f)
            def _():
                block[n, rows] = up[n, jnp.minimum(e, PANELS - 1)]

            @pl.when(f < e)
            def _():
                block[n, rows] = chosen[rows]

            @pl.when((e == f) & live)
            def _():
                block[n, rows] -= dot3((lh[rows], ll[rows]), (uh[n], ul[n]))

        stores[n].start()
    for n in range(2):
        stores[n].wait()


def pack_kernel(
    pivots, pattern, active, matrix, linv, uinv, mine, theirs, corner_mine, corner_theirs, side, alive,
    column, meets, lefts, right, sems, *, tile, last,
):
    xl, z, y, xh, core = place()
    piece, wide = tile // 8, 4 * tile
    q = middle_pivots(pivots, last)
    rows = [jnp.where(core == 0, 0, 3)] + [lax.rem(v, 4) for v in q]
    panel = [panel_of(pivots, v) for v in (jnp.where(core == 0, 0, last), *q)]
    panel = [jnp.minimum(p, PANELS - 1) for p in panel]
    early = [(matrix.at[:, pl.ds(0, tile)], column), (uinv.at[z], right)]
    for s in range(3):
        start = pl.multiple_of(rows[s] * tile, tile)
        early.append((matrix.at[pl.ds(start, tile), pl.ds(0, tile)], meets.at[s]))
        early.append((linv.at[panel[s]], lefts.at[s]))
    late = []
    outs = ((core, mine), (1 - core, theirs))
    for s in range(3):
        start = pl.multiple_of(rows[s] * tile, tile)
        for half, rows_out in outs:
            columns = pl.ds(pl.multiple_of(half * wide, wide), wide)
            late.append((matrix.at[pl.ds(start, tile), columns], rows_out.at[s, pl.ds(0, tile)]))
    copies = [pltpu.make_async_copy(*c, sems.at[n]) for n, c in enumerate(early + late)]
    for c in copies:
        c.start()
    for n in range(32):
        alive[n] = 0
    for n in range(active.shape[0]):
        alive[active[n, 0] * 8 + active[n, 1]] = 1
    sub = lax.broadcasted_iota(jnp.int32, (FLAG_ROWS, wide), 0)
    for half, rows_out in outs:
        block = lax.broadcasted_iota(jnp.int32, (FLAG_ROWS, wide), 1) // tile + half * 4
        for s in range(3):
            flags = jnp.zeros((FLAG_ROWS, wide), jnp.float32)
            for n in range(active.shape[0]):
                hit = (active[n, 0] == rows[s]) & (active[n, 1] == block) & (sub == 0)
                flags = jnp.where(hit, 1.0, flags)
            for n in range(PANELS):
                kind = jnp.where(pattern[rows[s], n] != 0, 1.0, 0.0)
                flags = jnp.where(sub == 1 + n, kind, flags)
            rows_out[s, tile:] = flags
    sub = lax.broadcasted_iota(jnp.int32, (FLAG_ROWS, tile), 0)
    flags = jnp.zeros((FLAG_ROWS, tile), jnp.float32)
    for n in range(active.shape[0]):
        flags = jnp.where((active[n, 0] == sub) & (active[n, 1] == 0), 1.0, flags)
    side[4 * tile :] = flags
    for s in range(3):
        first = jnp.where(core == 0, mine[s, tile:, :tile], theirs[s, tile:, :tile])
        for t in range(4):
            corner_mine[t, s, piece:] = first
            corner_theirs[t, s, piece:] = first
    for c in copies[: len(early)]:
        c.wait()
    side[: 4 * tile] = dot3(split(column[...]), split(right[...]))
    for s in range(3):

        @pl.when(panel[s] > z)
        def _():
            meets[s] = dot3(split(meets[s]), split(right[...]))

        @pl.when(panel[s] < z)
        def _():
            meets[s] = dot3(split(lefts[s]), split(meets[s]))

        for half in range(2):
            for t in range(4):
                value = meets[s, (half * 4 + t) * piece : (half * 4 + t + 1) * piece]

                @pl.when(core == half)
                def _():
                    corner_mine[t, s, :piece] = value

                @pl.when(core != half)
                def _():
                    corner_theirs[t, s, :piece] = value

    for c in copies[len(early) :]:
        c.wait()


def copy_one(out, index, options):
    for n, option in enumerate(options):

        @pl.when(index == n)
        def _():
            out[...] = option[...]


def cut_kernel(pivots, mine, theirs, own, *sends, tile, last, axis):
    _, _, y, xh, core = place()
    q = middle_pivots(pivots, last)
    near = [core == xh] + [lax.rem(v // 4, 2) == core for v in q]
    for d in range(4):
        t = lax.rem(y + d, 4)
        for s in range(3):
            if d == 0:
                out = own.at[s]
            else:
                out = sends[d - 1].at[s]
            at = (t, s) if axis == 0 else (s, slice(None), pl.ds(pl.multiple_of(t * tile, tile), tile))
            copy_one(out, jnp.where(near[s], 0, 1), [mine.at[at], theirs.at[at]])


def gather_kernel(pivots, own, *rest, last):
    _, _, y, xh, _ = place()
    q = middle_pivots(pivots, last)
    source = [3 * xh] + [v // 16 for v in q]
    out = rest[-1]
    for s in range(3):
        options = [own.at[s]] + [r.at[s] for r in rest[:3]]
        copy_one(out.at[s], lax.rem(y - source[s] + 4, 4), options)


def slots_of(pivots, last):
    _, _, _, xh, _ = place()
    q = middle_pivots(pivots, last)
    result = []
    for k in range(PANELS):
        p = pivots[k]
        which = jnp.where((p == 0) | (p == last), 0, jnp.where(p == q[0], 1, 2))
        result.append(which + jnp.where(lax.rem(p // 8, 2) == xh, 0, 3))
    return result


def order_kernel(pivots, mine, theirs, linv, out, *, tile, last):
    for k, slot in enumerate(slots_of(pivots, last)):
        copy_one(out.at[k], slot, [mine.at[s] for s in range(3)] + [theirs.at[s] for s in range(3)])
    for k in range(PANELS):
        out[k, :tile] = dot3(split(linv[k]), split(out[k, :tile]))


def order_corner_kernel(pivots, mine, theirs, out, *, piece, last):
    z = place()[1]
    for k, slot in enumerate(slots_of(pivots, last)):
        for n in range(6):
            source = (mine if n < 3 else theirs).at[n % 3]

            @pl.when((slot == n) & (z != k))
            def _():
                at = pl.multiple_of((k - jnp.where(z < k, 1, 0)) * piece, 8)
                out[pl.ds(at, piece)] = source[:piece]

            @pl.when(slot == n)
            def _():
                at = (PANELS - 1) * piece + k
                out[at : at + 1] = source[piece : piece + 1]
                out[at + PANELS : at + PANELS + 1] = source[pl.ds(piece + 1 + z, 1)]


VMEM = pl.BlockSpec(memory_space=pltpu.VMEM)
SMEM = pl.BlockSpec(memory_space=pltpu.SMEM)
ANY = pl.BlockSpec(memory_space=pl.ANY)
HBM = pl.BlockSpec(memory_space=pltpu.HBM)
LITTLE = pl.CostEstimate(flops=1000, bytes_accessed=1000, transcendentals=0)


def small(kernel, pivots, arrays, shapes, **sizes):
    return pl.pallas_call(
        functools.partial(kernel, **sizes),
        in_specs=[SMEM] + [VMEM] * len(arrays),
        out_specs=[VMEM] * len(shapes),
        out_shape=[jax.ShapeDtypeStruct(s, jnp.float32) for s in shapes],
        compiler_params=pltpu.CompilerParams(vmem_limit_bytes=24 * MIB),
        cost_estimate=LITTLE,
    )(pivots, *arrays)


def pack(pivots, pattern, active, matrix, linv, uinv, tile, last):
    def shape(*dims):
        return jax.ShapeDtypeStruct(dims, jnp.float32)

    rows = shape(3, tile + FLAG_ROWS, 4 * tile)
    pieces = shape(4, 3, tile // 8 + FLAG_ROWS, tile)
    alive = jax.ShapeDtypeStruct((32,), jnp.int32)
    return pl.pallas_call(
        functools.partial(pack_kernel, tile=tile, last=last),
        in_specs=[SMEM] * 3 + [HBM] * 3,
        out_specs=[VMEM] * 5 + [SMEM],
        out_shape=[rows, rows, pieces, pieces, shape(4 * tile + FLAG_ROWS, tile), alive],
        scratch_shapes=[
            pltpu.VMEM((4 * tile, tile), jnp.float32),
            pltpu.VMEM((3, tile, tile), jnp.float32),
            pltpu.VMEM((3, tile, tile), jnp.float32),
            pltpu.VMEM((tile, tile), jnp.float32),
            pltpu.SemaphoreType.DMA((14,)),
        ],
        compiler_params=pltpu.CompilerParams(vmem_limit_bytes=56 * MIB),
        cost_estimate=LITTLE,
    )(pivots, pattern, active, matrix, linv, uinv)


def lower_part(pivots, pattern, sides, corner, linv, uinv, tile):
    given = (*sides, *corner, linv, uinv)
    six = jax.ShapeDtypeStruct((len(PAIRS), tile, tile), jnp.bfloat16)
    big = jax.ShapeDtypeStruct((4 * tile, PANELS * tile), jnp.bfloat16)
    return pl.pallas_call(
        functools.partial(lower_kernel, tile=tile),
        in_specs=[SMEM] * 2 + [ANY] * 8,
        out_specs=[VMEM] * 5,
        out_shape=[big, big, jax.ShapeDtypeStruct((4 * tile, tile), jnp.float32), six, six],
        scratch_shapes=[pltpu.VMEM(x.shape, x.dtype) for x in given] + [pltpu.SemaphoreType.DMA((len(given),))],
        compiler_params=pltpu.CompilerParams(vmem_limit_bytes=40 * MIB),
        cost_estimate=pl.CostEstimate(flops=6 * 10**9, bytes_accessed=20 * MIB, transcendentals=0),
    )(pivots, pattern, *given)


def update_part(pivots, alive, raw_a, raw_b, lower, old, partial, tile, distance):
    given = [] if partial is None else [partial]
    return pl.pallas_call(
        functools.partial(update_kernel, tile=tile, distance=distance, parts=len(raw_a)),
        in_specs=[SMEM] * 2 + [VMEM] * (5 + 2 * len(raw_a)) + [HBM] * (1 + len(given)),
        out_specs=HBM,
        out_shape=jax.ShapeDtypeStruct(old.shape, old.dtype),
        scratch_shapes=[
            pltpu.VMEM((2, 4 * tile, tile), jnp.float32),
            pltpu.VMEM((2, PANELS, tile, tile), jnp.float32),
            pltpu.VMEM((2, PANELS * tile, tile), jnp.bfloat16),
            pltpu.VMEM((2, PANELS * tile, tile), jnp.bfloat16),
            pltpu.SemaphoreType.DMA((4,)),
        ],
        input_output_aliases={8 + 2 * len(raw_a): 0} if given else {},
        compiler_params=pltpu.CompilerParams(vmem_limit_bytes=40 * MIB),
        cost_estimate=pl.CostEstimate(flops=5 * 10**9, bytes_accessed=8 * MIB, transcendentals=0),
    )(pivots, alive, *raw_a, *raw_b, *lower, old, *given)


def turn(x, axis, distance):
    return lax.ppermute(x, axis, [(i, (i + distance) % 4) for i in range(4)])


def swap(x, axis):
    return lax.ppermute(x, axis, [(0, 1), (1, 0)])


def pick(index, options):
    result = options[-1]
    for i in range(len(options) - 2, -1, -1):
        result = jnp.where(index == i, options[i], result)
    return result


def after(x, *others):
    return lax.optimization_barrier((x, others))[0]


def body(matrix, pattern, active, pivots, lower_inv, upper_inv):
    tile = lower_inv.shape[1]
    piece = tile // 8
    xl = lax.axis_index("xl")
    last = 16 * 4 - 1
    packed = pack(pivots, pattern, active[0, 0], matrix, lower_inv, upper_inv, tile, last)
    rows_mine, rows_theirs, corner_mine, corner_theirs, side, alive = packed

    corner_theirs = swap(corner_theirs, "core")
    rows_theirs = swap(rows_theirs, "core")
    side_far = lax.ppermute(side, "xl", [(0, 1)])
    small_slots = (3, piece + FLAG_ROWS, tile)
    own_c, *sends_c = small(
        cut_kernel, pivots, (corner_mine, corner_theirs), [small_slots] * 4, tile=tile, last=last, axis=0
    )
    recv_c = [turn(x, "y", d + 1) for d, x in enumerate(sends_c)]
    (slots_c,) = small(gather_kernel, pivots, (own_c, *recv_c), [small_slots], last=last)
    side = jnp.where(xl == 0, side, after(side_far, slots_c))
    near = [turn(side, "z", 1), turn(side, "z", 3)]
    (corner,) = small(
        order_corner_kernel,
        pivots,
        (after(slots_c, side), swap(slots_c, "xh")),
        [(3 * piece + FLAG_ROWS, tile)],
        piece=piece,
        last=last,
    )
    corner, rows_theirs = lax.optimization_barrier((corner, rows_theirs))
    corner_y = jnp.stack([corner] + [turn(corner, "y", d) for d in range(1, 4)])

    one = (tile + FLAG_ROWS, tile)
    own, *sends = small(
        cut_kernel, pivots, (after(rows_mine, corner_y), rows_theirs), [(3, *one)] * 4, tile=tile, last=last, axis=2
    )
    corner_y = jnp.where(xl == 0, corner_y, lax.ppermute(corner_y, "xl", [(0, 1)]))
    sends[1] = after(sends[1], *near)
    recv = [turn(x, "y", d + 1) for d, x in enumerate(sends)]
    corner_y = after(corner_y, recv[0], recv[2])
    corner_z = [corner_y] + [turn(corner_y, "z", d) for d in range(1, 4)]
    far = turn(after(side, *near), "z", 2)
    (slots,) = small(gather_kernel, pivots, (own, *recv), [(3, *one)], last=last)
    other_slots = swap(slots, "xh")
    (item,) = small(
        order_kernel, pivots, (after(slots, far, *corner_z), other_slots, lower_inv), [(4, *one)], tile=tile, last=last
    )
    corner_z = jnp.stack(corner_z)
    sides = [side, near[0], far, near[1]]
    items = [[item], [turn(item, "y", 1)], None, [turn(item, "y", 3)]]
    lower = lower_part(pivots, pattern, sides, (corner_z, swap(corner_z, "core")), lower_inv, upper_inv, tile)
    def update(d, mine, other, out):
        return update_part(pivots, alive, mine, other, lower, matrix, out, tile, d)

    out = update(0, items[0], [swap(item, "core")], None)
    items[1], items[3] = after(items[1], out), after(items[3], out)
    items[2] = [turn(items[1][0][:2], "y", 1), turn(items[3][0][2:], "y", 3)]
    others = {d: [swap(x, "core") for x in items[d]] for d in (1, 3)}
    out = update(1, items[1], others[1], out)
    out = update(3, items[3], others[3], out)
    items[2] = after(items[2], out)
    others[2] = [swap(x, "core") for x in items[2]]
    return update(2, items[2], others[2], out)


def solution(mesh):
    fine = Mesh(mesh.devices.reshape(2, 4, 4, 2, 2), ("xl", "z", "y", "xh", "core"))
    row, col = ("y", "xh", "core"), ("xl", "z")
    in_specs = (P(row, col), P(row, None), P(row, col, None, None), P(), P(), P())
    return jax.shard_map(body, mesh=fine, in_specs=in_specs, out_specs=P(row, col), check_vma=False)
```

```python
import functools

import jax
import jax.numpy as jnp
from jax import lax
from jax.experimental import pallas as pl
from jax.experimental.pallas import tpu as pltpu
from jax.sharding import Mesh, PartitionSpec as P

PANELS = 4
PAIRS = [(m, p) for m in range(PANELS) for p in range(m + 1, PANELS)]
FLAG_ROWS = 8
MIB = 1024 * 1024


def split(x):
    high = x.astype(jnp.bfloat16)
    return high, (x - high.astype(jnp.float32)).astype(jnp.bfloat16)


def dot3(a, b):
    dot = functools.partial(jnp.dot, preferred_element_type=jnp.float32)
    return dot(a[0], b[0]) + (dot(a[0], b[1]) + dot(a[1], b[0]))


def place():
    return tuple(lax.axis_index(n) for n in ("xl", "z", "y", "xh", "core"))


def middle_pivots(pivots, last):
    first = second = jnp.int32(-1)
    for k in range(PANELS):
        p = pivots[k]
        inside = (p != 0) & (p != last)
        second = jnp.where(inside & (first >= 0), p, second)
        first = jnp.where(inside & (first < 0), p, first)
    return first, second


def panel_of(pivots, row):
    result = jnp.int32(PANELS)
    for k in range(PANELS - 1, -1, -1):
        result = jnp.where(pivots[k] == row, k, result)
    return result


def lower_kernel(pivots, pattern, *refs, tile):
    given, (lh, ll, chosen, ch, cl), held, sems = refs[:8], refs[8:13], refs[13:21], refs[21]
    copies = [pltpu.make_async_copy(g, h, sems.at[n]) for n, (g, h) in enumerate(zip(given, held))]
    for n in (4, 5, 6, 7, 0, 1, 2, 3):
        copies[n].start()
    raw0, raw1, raw2, raw3, mine, theirs, linv, uinv = held
    xl, z, y, xh, core = place()
    b = xl * 4 + z
    ends = [panel_of(pivots, ((y * 2 + xh) * 2 + core) * 4 + l) for l in range(4)]
    piece = tile // 8

    def corner_tile(k, m):
        def rows(c):
            at = pl.ds((m - (m > k)) * piece, piece)
            dz = lax.rem(z - k + 4, 4)
            near = jnp.concatenate([mine[dz, lax.rem(y - t + 4, 4), at] for t in range(4)], axis=0)
            far = jnp.concatenate([theirs[dz, lax.rem(y - t + 4, 4), at] for t in range(4)], axis=0)
            return jnp.where(core == c, near, far)

        return jnp.concatenate([rows(0), rows(1)], axis=0)

    def corner_flag(k, row):
        at = (PANELS - 1) * piece + row
        return mine[lax.rem(z - k + 4, 4), 0, at : at + 1]

    for n in range(4, 8):
        copies[n].wait()
    uinvs = [split(uinv[k]) for k in range(PANELS)]
    linvs = [split(linv[k]) for k in range(PANELS)]
    pairs = [(m, p) for m in range(PANELS) for p in range(m + 1, PANELS)]
    high = {(m, c): corner_tile(c, m) for m, c in pairs}
    wide = {(m, p): corner_tile(m, p) for m, p in pairs}
    low, up, left, right = {}, {}, {}, {}
    for m in range(PANELS - 1):
        for n in range(m + 1, PANELS):
            u, l = high[m, n], wide[m, n]
            if m:
                u = u - corner_flag(n, m) * sum(dot3(left[r, m], up[r, n]) for r in range(m))
                l = l - corner_flag(m, n) * sum(dot3(low[r, n], right[r, m]) for r in range(m))
            up[m, n] = split(u)
            low[m, n] = split(l * corner_flag(m, PANELS + n))
        for n in range(m + 1, PANELS):
            left[m, n] = split(dot3(linvs[n], low[m, n]))
            right[m, n] = split(dot3(up[m, n], uinvs[n]))
            at = PAIRS.index((m, n))
            ch[at], cl[at] = left[m, n]

    def choose(at, rows):
        return pick(at, [raw[rows] for raw in (raw0, raw1, raw2, raw3)])

    def by_row(values):
        return jnp.concatenate([jnp.broadcast_to(v, (tile, tile)) for v in values], axis=0)

    for n in range(4):
        copies[n].wait()
    done = []
    for k in range(PANELS):
        at = lax.rem(z - k + 4, 4)
        value = choose(at, slice(0, 4 * tile))
        if k:
            flag = by_row([choose(at, slice(4 * tile + l, 4 * tile + l + 1)) for l in range(4)])
            value = value - flag * sum(dot3(done[m], right[m, k]) for m in range(k))
        here = [(pattern[l, k] != 0) & (ends[l] > k) for l in range(4)]
        value = jnp.concatenate(
            [jnp.where(here[l], value[l * tile : (l + 1) * tile], 0.0) for l in range(4)], axis=0
        )
        done.append(split(value))
        columns = slice(k * tile, (k + 1) * tile)
        lh[:, columns], ll[:, columns] = done[-1]

        @pl.when(b == k)
        def _():
            chosen[...] = value


def update_kernel(pivots, alive, *refs, tile, distance, parts):
    raw_a, raw_b = refs[:parts], refs[parts : 2 * parts]
    lh, ll, chosen, ch, cl, old = refs[2 * parts : 2 * parts + 6]
    rest = refs[2 * parts + 6 :]
    each = PANELS // parts
    xl, z, y, xh, core = place()
    b, t = xl * 4 + z, lax.rem(y + 4 - distance, 4)
    js = [core * 4 + t, (1 - core) * 4 + t]
    fs = [jnp.where((j == 0) & (b < PANELS), b, PANELS) for j in js]
    ends = [panel_of(pivots, ((y * 2 + xh) * 2 + core) * 4 + l) for l in range(4)]
    new, block, up, uh, ul, sems = rest[-6:]
    loads, stores = [], []
    for n in range(2):
        columns = pl.ds(pl.multiple_of(js[n] * tile, tile), tile)
        loads.append(pltpu.make_async_copy(old.at[:, columns], block.at[n], sems.at[n]))
        stores.append(pltpu.make_async_copy(block.at[n], new.at[:, columns], sems.at[2 + n]))
        loads[n].start()
    done = []
    for k in range(PANELS):
        pair = [raw[k // each].at[k % each] for raw in (raw_a, raw_b)]
        value = jnp.concatenate([r[:tile] for r in pair], axis=1)
        if k:
            at = [PAIRS.index((m, k)) for m in range(k)]
            total = sum(dot3((ch[at[m]], cl[at[m]]), done[m]) for m in range(k))
            value = value - jnp.concatenate([r[tile : tile + 1] for r in pair], axis=1) * total
        done.append(split(value))
        rows = slice(k * tile, (k + 1) * tile)
        for n in range(2):
            columns = slice(n * tile, (n + 1) * tile)
            used = k < fs[n]
            up[n, k] = value[:, columns]
            uh[n, rows] = jnp.where(used, done[-1][0][:, columns], jnp.zeros((), jnp.bfloat16))
            ul[n, rows] = jnp.where(used, done[-1][1][:, columns], jnp.zeros((), jnp.bfloat16))
    for n in range(2):
        loads[n].wait()
        f = fs[n]
        for l in range(4):
            rows = slice(l * tile, (l + 1) * tile)
            e, live = ends[l], alive[l * 8 + js[n]] != 0

            @pl.when(e < f)
            def _():
                block[n, rows] = up[n, jnp.minimum(e, PANELS - 1)]

            @pl.when(f < e)
            def _():
                block[n, rows] = chosen[rows]

            @pl.when((e == f) & live)
            def _():
                block[n, rows] -= dot3((lh[rows], ll[rows]), (uh[n], ul[n]))

        stores[n].start()
    for n in range(2):
        stores[n].wait()


def pack_kernel(
    pivots, pattern, active, matrix, linv, uinv, mine, theirs, corner_mine, corner_theirs, side, alive,
    column, meets, lefts, right, sems, *, tile, last,
):
    xl, z, y, xh, core = place()
    piece, wide = tile // 8, 4 * tile
    q = middle_pivots(pivots, last)
    rows = [jnp.where(core == 0, 0, 3)] + [lax.rem(v, 4) for v in q]
    panel = [panel_of(pivots, v) for v in (jnp.where(core == 0, 0, last), *q)]
    panel = [jnp.minimum(p, PANELS - 1) for p in panel]
    early = [(matrix.at[:, pl.ds(0, tile)], column), (uinv.at[z], right)]
    for s in range(3):
        start = pl.multiple_of(rows[s] * tile, tile)
        early.append((matrix.at[pl.ds(start, tile), pl.ds(0, tile)], meets.at[s]))
        early.append((linv.at[panel[s]], lefts.at[s]))
    late = []
    outs = ((core, mine), (1 - core, theirs))
    for s in range(3):
        start = pl.multiple_of(rows[s] * tile, tile)
        for half, rows_out in outs:
            columns = pl.ds(pl.multiple_of(half * wide, wide), wide)
            late.append((matrix.at[pl.ds(start, tile), columns], rows_out.at[s, pl.ds(0, tile)]))
    copies = [pltpu.make_async_copy(*c, sems.at[n]) for n, c in enumerate(early + late)]
    for c in copies:
        c.start()
    for n in range(32):
        alive[n] = 0
    for n in range(active.shape[0]):
        alive[active[n, 0] * 8 + active[n, 1]] = 1
    sub = lax.broadcasted_iota(jnp.int32, (FLAG_ROWS, wide), 0)
    for half, rows_out in outs:
        block = lax.broadcasted_iota(jnp.int32, (FLAG_ROWS, wide), 1) // tile + half * 4
        for s in range(3):
            flags = jnp.zeros((FLAG_ROWS, wide), jnp.float32)
            for n in range(active.shape[0]):
                hit = (active[n, 0] == rows[s]) & (active[n, 1] == block) & (sub == 0)
                flags = jnp.where(hit, 1.0, flags)
            for n in range(PANELS):
                kind = jnp.where(pattern[rows[s], n] != 0, 1.0, 0.0)
                flags = jnp.where(sub == 1 + n, kind, flags)
            rows_out[s, tile:] = flags
    sub = lax.broadcasted_iota(jnp.int32, (FLAG_ROWS, tile), 0)
    flags = jnp.zeros((FLAG_ROWS, tile), jnp.float32)
    for n in range(active.shape[0]):
        flags = jnp.where((active[n, 0] == sub) & (active[n, 1] == 0), 1.0, flags)
    side[4 * tile :] = flags
    for s in range(3):
        first = jnp.where(core == 0, mine[s, tile:, :tile], theirs[s, tile:, :tile])
        for t in range(4):
            corner_mine[t, s, piece:] = first
            corner_theirs[t, s, piece:] = first
    for c in copies[: len(early)]:
        c.wait()
    side[: 4 * tile] = dot3(split(column[...]), split(right[...]))
    for s in range(3):

        @pl.when(panel[s] > z)
        def _():
            meets[s] = dot3(split(meets[s]), split(right[...]))

        @pl.when(panel[s] < z)
        def _():
            meets[s] = dot3(split(lefts[s]), split(meets[s]))

        for half in range(2):
            for t in range(4):
                value = meets[s, (half * 4 + t) * piece : (half * 4 + t + 1) * piece]

                @pl.when(core == half)
                def _():
                    corner_mine[t, s, :piece] = value

                @pl.when(core != half)
                def _():
                    corner_theirs[t, s, :piece] = value

    for c in copies[len(early) :]:
        c.wait()


def copy_one(out, index, options):
    for n, option in enumerate(options):

        @pl.when(index == n)
        def _():
            out[...] = option[...]


def cut_kernel(pivots, mine, theirs, own, *sends, tile, last, axis):
    _, _, y, xh, core = place()
    q = middle_pivots(pivots, last)
    near = [core == xh] + [lax.rem(v // 4, 2) == core for v in q]
    for d in range(4):
        t = lax.rem(y + d, 4)
        for s in range(3):
            if d == 0:
                out = own.at[s]
            else:
                out = sends[d - 1].at[s]
            at = (t, s) if axis == 0 else (s, slice(None), pl.ds(pl.multiple_of(t * tile, tile), tile))
            copy_one(out, jnp.where(near[s], 0, 1), [mine.at[at], theirs.at[at]])


def gather_kernel(pivots, own, *rest, last):
    _, _, y, xh, _ = place()
    q = middle_pivots(pivots, last)
    source = [3 * xh] + [v // 16 for v in q]
    out = rest[-1]
    for s in range(3):
        options = [own.at[s]] + [r.at[s] for r in rest[:3]]
        copy_one(out.at[s], lax.rem(y - source[s] + 4, 4), options)


def slots_of(pivots, last):
    _, _, _, xh, _ = place()
    q = middle_pivots(pivots, last)
    result = []
    for k in range(PANELS):
        p = pivots[k]
        which = jnp.where((p == 0) | (p == last), 0, jnp.where(p == q[0], 1, 2))
        result.append(which + jnp.where(lax.rem(p // 8, 2) == xh, 0, 3))
    return result


def order_kernel(pivots, mine, theirs, linv, out, *, tile, last):
    for k, slot in enumerate(slots_of(pivots, last)):
        copy_one(out.at[k], slot, [mine.at[s] for s in range(3)] + [theirs.at[s] for s in range(3)])
    for k in range(PANELS):
        out[k, :tile] = dot3(split(linv[k]), split(out[k, :tile]))


def order_corner_kernel(pivots, mine, theirs, out, *, piece, last):
    z = place()[1]
    for k, slot in enumerate(slots_of(pivots, last)):
        for n in range(6):
            source = (mine if n < 3 else theirs).at[n % 3]

            @pl.when((slot == n) & (z != k))
            def _():
                at = pl.multiple_of((k - jnp.where(z < k, 1, 0)) * piece, 8)
                out[pl.ds(at, piece)] = source[:piece]

            @pl.when(slot == n)
            def _():
                at = (PANELS - 1) * piece + k
                out[at : at + 1] = source[piece : piece + 1]
                out[at + PANELS : at + PANELS + 1] = source[pl.ds(piece + 1 + z, 1)]


VMEM = pl.BlockSpec(memory_space=pltpu.VMEM)
SMEM = pl.BlockSpec(memory_space=pltpu.SMEM)
ANY = pl.BlockSpec(memory_space=pl.ANY)
HBM = pl.BlockSpec(memory_space=pltpu.HBM)
LITTLE = pl.CostEstimate(flops=1000, bytes_accessed=1000, transcendentals=0)


def small(kernel, pivots, arrays, shapes, **sizes):
    return pl.pallas_call(
        functools.partial(kernel, **sizes),
        in_specs=[SMEM] + [VMEM] * len(arrays),
        out_specs=[VMEM] * len(shapes),
        out_shape=[jax.ShapeDtypeStruct(s, jnp.float32) for s in shapes],
        compiler_params=pltpu.CompilerParams(vmem_limit_bytes=24 * MIB),
        cost_estimate=LITTLE,
    )(pivots, *arrays)


def pack(pivots, pattern, active, matrix, linv, uinv, tile, last):
    def shape(*dims):
        return jax.ShapeDtypeStruct(dims, jnp.float32)

    rows = shape(3, tile + FLAG_ROWS, 4 * tile)
    pieces = shape(4, 3, tile // 8 + FLAG_ROWS, tile)
    alive = jax.ShapeDtypeStruct((32,), jnp.int32)
    return pl.pallas_call(
        functools.partial(pack_kernel, tile=tile, last=last),
        in_specs=[SMEM] * 3 + [HBM] * 3,
        out_specs=[VMEM] * 5 + [SMEM],
        out_shape=[rows, rows, pieces, pieces, shape(4 * tile + FLAG_ROWS, tile), alive],
        scratch_shapes=[
            pltpu.VMEM((4 * tile, tile), jnp.float32),
            pltpu.VMEM((3, tile, tile), jnp.float32),
            pltpu.VMEM((3, tile, tile), jnp.float32),
            pltpu.VMEM((tile, tile), jnp.float32),
            pltpu.SemaphoreType.DMA((14,)),
        ],
        compiler_params=pltpu.CompilerParams(vmem_limit_bytes=56 * MIB),
        cost_estimate=LITTLE,
    )(pivots, pattern, active, matrix, linv, uinv)


def lower_part(pivots, pattern, sides, corner, linv, uinv, tile):
    given = (*sides, *corner, linv, uinv)
    six = jax.ShapeDtypeStruct((len(PAIRS), tile, tile), jnp.bfloat16)
    big = jax.ShapeDtypeStruct((4 * tile, PANELS * tile), jnp.bfloat16)
    return pl.pallas_call(
        functools.partial(lower_kernel, tile=tile),
        in_specs=[SMEM] * 2 + [ANY] * 8,
        out_specs=[VMEM] * 5,
        out_shape=[big, big, jax.ShapeDtypeStruct((4 * tile, tile), jnp.float32), six, six],
        scratch_shapes=[pltpu.VMEM(x.shape, x.dtype) for x in given] + [pltpu.SemaphoreType.DMA((len(given),))],
        compiler_params=pltpu.CompilerParams(vmem_limit_bytes=40 * MIB),
        cost_estimate=pl.CostEstimate(flops=6 * 10**9, bytes_accessed=20 * MIB, transcendentals=0),
    )(pivots, pattern, *given)


def update_part(pivots, alive, raw_a, raw_b, lower, old, partial, tile, distance):
    given = [] if partial is None else [partial]
    return pl.pallas_call(
        functools.partial(update_kernel, tile=tile, distance=distance, parts=len(raw_a)),
        in_specs=[SMEM] * 2 + [VMEM] * (5 + 2 * len(raw_a)) + [HBM] * (1 + len(given)),
        out_specs=HBM,
        out_shape=jax.ShapeDtypeStruct(old.shape, old.dtype),
        scratch_shapes=[
            pltpu.VMEM((2, 4 * tile, tile), jnp.float32),
            pltpu.VMEM((2, PANELS, tile, tile), jnp.float32),
            pltpu.VMEM((2, PANELS * tile, tile), jnp.bfloat16),
            pltpu.VMEM((2, PANELS * tile, tile), jnp.bfloat16),
            pltpu.SemaphoreType.DMA((4,)),
        ],
        input_output_aliases={8 + 2 * len(raw_a): 0} if given else {},
        compiler_params=pltpu.CompilerParams(vmem_limit_bytes=40 * MIB),
        cost_estimate=pl.CostEstimate(flops=5 * 10**9, bytes_accessed=8 * MIB, transcendentals=0),
    )(pivots, alive, *raw_a, *raw_b, *lower, old, *given)


def turn(x, axis, distance):
    return lax.ppermute(x, axis, [(i, (i + distance) % 4) for i in range(4)])


def swap(x, axis):
    return lax.ppermute(x, axis, [(0, 1), (1, 0)])


def pick(index, options):
    result = options[-1]
    for i in range(len(options) - 2, -1, -1):
        result = jnp.where(index == i, options[i], result)
    return result


def after(x, *others):
    return lax.optimization_barrier((x, others))[0]


def body(matrix, pattern, active, pivots, lower_inv, upper_inv):
    tile = lower_inv.shape[1]
    piece = tile // 8
    xl = lax.axis_index("xl")
    last = 16 * 4 - 1
    packed = pack(pivots, pattern, active[0, 0], matrix, lower_inv, upper_inv, tile, last)
    rows_mine, rows_theirs, corner_mine, corner_theirs, side, alive = packed

    corner_theirs = swap(corner_theirs, "core")
    rows_theirs = swap(rows_theirs, "core")
    side_far = lax.ppermute(side, "xl", [(0, 1)])
    small_slots = (3, piece + FLAG_ROWS, tile)
    own_c, *sends_c = small(
        cut_kernel, pivots, (corner_mine, corner_theirs), [small_slots] * 4, tile=tile, last=last, axis=0
    )
    recv_c = [turn(x, "y", d + 1) for d, x in enumerate(sends_c)]
    (slots_c,) = small(gather_kernel, pivots, (own_c, *recv_c), [small_slots], last=last)
    side = jnp.where(xl == 0, side, after(side_far, slots_c))
    near = [turn(side, "z", 1), turn(side, "z", 3)]
    (corner,) = small(
        order_corner_kernel,
        pivots,
        (after(slots_c, side), swap(slots_c, "xh")),
        [(3 * piece + FLAG_ROWS, tile)],
        piece=piece,
        last=last,
    )
    corner, rows_theirs = lax.optimization_barrier((corner, rows_theirs))
    corner_y = jnp.stack([corner] + [turn(corner, "y", d) for d in range(1, 4)])

    one = (tile + FLAG_ROWS, tile)
    own, *sends = small(
        cut_kernel, pivots, (after(rows_mine, corner_y), rows_theirs), [(3, *one)] * 4, tile=tile, last=last, axis=2
    )
    corner_y = jnp.where(xl == 0, corner_y, lax.ppermute(corner_y, "xl", [(0, 1)]))
    sends[1] = after(sends[1], corner_y)
    recv = [turn(x, "y", d + 1) for d, x in enumerate(sends)]
    corner_y = after(corner_y, recv[0], recv[2], *near)
    corner_z = [corner_y] + [turn(corner_y, "z", d) for d in range(1, 4)]
    far = turn(after(side, *near), "z", 2)
    (slots,) = small(gather_kernel, pivots, (own, *recv), [(3, *one)], last=last)
    other_slots = swap(slots, "xh")
    (item,) = small(
        order_kernel, pivots, (after(slots, *corner_z), other_slots, lower_inv), [(4, *one)], tile=tile, last=last
    )
    corner_z = jnp.stack(corner_z)
    sides = [side, near[0], far, near[1]]
    items = [[item], [turn(item, "y", 1)], None, [turn(item, "y", 3)]]
    lower = lower_part(pivots, pattern, sides, (corner_z, swap(corner_z, "core")), lower_inv, upper_inv, tile)
    def update(d, mine, other, out):
        return update_part(pivots, alive, mine, other, lower, matrix, out, tile, d)

    out = update(0, items[0], [swap(item, "core")], None)
    items[1], items[3] = after(items[1], out), after(items[3], out)
    items[2] = [turn(items[1][0][:2], "y", 1), turn(items[3][0][2:], "y", 3)]
    others = {d: [swap(x, "core") for x in items[d]] for d in (1, 3)}
    out = update(1, items[1], others[1], out)
    out = update(3, items[3], others[3], out)
    items[2] = after(items[2], out)
    others[2] = [swap(x, "core") for x in items[2]]
    return update(2, items[2], others[2], out)


def solution(mesh):
    fine = Mesh(mesh.devices.reshape(2, 4, 4, 2, 2), ("xl", "z", "y", "xh", "core"))
    row, col = ("y", "xh", "core"), ("xl", "z")
    in_specs = (P(row, col), P(row, None), P(row, col, None, None), P(), P(), P())
    return jax.shard_map(body, mesh=fine, in_specs=in_specs, out_specs=P(row, col), check_vma=False)
```
